256 devices in a mesh: row: 16 (over x, y), col: 16 (over z, core).
Axes of the slice: x: 4, y: 4, z: 8, core: 2. Of those that a mesh axis runs over, the one named last changes fastest.
Arguments:
- tokens: bfloat16 [512, 12288], P('col', 'row'), may hold values from -6 to 6
- weight_in: bfloat16 [12288, 24576], P('row', 'col'), may hold values from -0.0546875 to 0.0546875
- weight_out: bfloat16 [24576, 12288], P('col', 'row'), may hold values from -0.0390625 to 0.0390625
- cotangent: bfloat16 [512, 12288], P('col', 'row'), may hold values from -6 to 6
Outputs:
- output: bfloat16 [512, 12288], P('col', 'row')
- grad_tokens: bfloat16 [512, 12288], P('col', 'row')
- grad_in: bfloat16 [12288, 24576], P('row', 'col')
- grad_out: bfloat16 [24576, 12288], P('col', 'row')
The draws below stay inside these ranges and needn't reach their ends.
All inputs are finite; a program needn't handle non-finite values.
Results may differ from the reference program's by a relative error of at most 0.034.
Values may be sent and summed in bfloat16 or wider, within the bound.
No kernel may reach another device: no remote copies, remote signals or barrier semaphores. Data moves between devices by JAX's collectives and lax.ppermute only.
A program may use at most 64 MiB of HBM per device.

```python
import jax
import jax.numpy as jnp
from jax import lax

D = 12288
FF = 24576
TOKENS = 512
N_ROW = 16
N_COL = 16


def block_scale(rng, shape, split, low, largest):
    def one(dim, parts):
        heights = jax.random.uniform(jax.random.fold_in(jax.random.fold_in(rng, 6), dim), (parts,), jnp.float32, low / len(split), largest / len(split))
        return jnp.repeat(jnp.exp(heights), shape[dim] // parts).reshape((-1,) + (1,) * (len(shape) - dim - 1))

    gain = one(*split[0])
    for cut in split[1:]:
        gain = gain * one(*cut)
    return gain


def centred(stream_key, dims, width, limit, split=(), kind=jnp.bfloat16):
    drawn = width * jax.random.normal(stream_key, dims, jnp.float32)
    if split:
        drawn = drawn * block_scale(stream_key, dims, split, -0.22, 0.18)
    return jnp.clip(drawn, -limit, limit).astype(kind)


def setup_inputs(seed: int = 0) -> dict:
    seeds = jax.random.split(jax.random.key(seed), 5)
    return {
        "tokens": centred(seeds[0], (TOKENS, D), 1.0, 6.0, ((0, 16), (1, 16))),
        "weight_in": centred(seeds[1], (D, FF), D ** -0.5, 0.0546875, ((0, 16), (1, 16))),
        "weight_out": centred(seeds[2], (FF, D), FF ** -0.5, 0.0390625, ((0, 16), (1, 16))),
        "cotangent": centred(seeds[3], (TOKENS, D), 1.0, 6.0, ((0, 16), (1, 16))),
    }


tanh_gain = 0.7978845608028654
cubic_term = 0.044715


def gelu_value(hidden):
    return 0.5 * hidden * (1.0 + jnp.tanh(tanh_gain * (hidden + cubic_term * hidden * hidden * hidden)))


def gelu_slope(hidden):
    squared = hidden * hidden
    tangent = jnp.tanh(tanh_gain * (hidden + cubic_term * squared * hidden))
    return 0.5 * (1.0 + tangent) + 0.5 * hidden * (1.0 - tangent * tangent) * tanh_gain * (1.0 + 3.0 * cubic_term * squared)


def rounded_sum(term_of, blocks, shape):
    def accumulate(block_index, running):
        rounded = lax.optimization_barrier(term_of(block_index).astype(jnp.bfloat16))
        return running + rounded.astype(jnp.float32)
    return lax.fori_loop(0, blocks, accumulate, jnp.zeros(shape, jnp.float32))


def reference(tokens, weight_in, weight_out, cotangent):
    model_block = D // N_ROW
    hidden_block = FF // N_COL
    grad_scale = TOKENS ** -0.5

    def hidden_term(block_index):
        begin = (block_index * model_block).astype(jnp.int32)
        left = lax.dynamic_slice_in_dim(tokens, begin, model_block, 1)
        right = lax.dynamic_slice_in_dim(weight_in, begin, model_block, 0)
        return jnp.dot(left, right, preferred_element_type=jnp.float32)

    hidden = rounded_sum(hidden_term, N_ROW, (TOKENS, FF))
    activation = gelu_value(hidden).astype(jnp.bfloat16)

    def output_term(block_index):
        begin = (block_index * hidden_block).astype(jnp.int32)
        left = lax.dynamic_slice_in_dim(activation, begin, hidden_block, 1)
        right = lax.dynamic_slice_in_dim(weight_out, begin, hidden_block, 0)
        return jnp.dot(left, right, preferred_element_type=jnp.float32)

    output = rounded_sum(output_term, N_COL, (TOKENS, D)).astype(jnp.bfloat16)
    grad_out = (jnp.dot(activation.T, cotangent, preferred_element_type=jnp.float32) * grad_scale).astype(jnp.bfloat16)

    def grad_term(block_index):
        begin = (block_index * model_block).astype(jnp.int32)
        left = lax.dynamic_slice_in_dim(cotangent, begin, model_block, 1)
        right = lax.dynamic_slice_in_dim(weight_out, begin, model_block, 1)
        return jnp.dot(left, right.T, preferred_element_type=jnp.float32)

    grad_activation = rounded_sum(grad_term, N_ROW, (TOKENS, FF))
    grad_hidden = (grad_activation * gelu_slope(hidden)).astype(jnp.bfloat16)
    grad_in = (jnp.dot(tokens.T, grad_hidden, preferred_element_type=jnp.float32) * grad_scale).astype(jnp.bfloat16)

    def input_term(block_index):
        begin = (block_index * hidden_block).astype(jnp.int32)
        left = lax.dynamic_slice_in_dim(grad_hidden, begin, hidden_block, 1)
        right = lax.dynamic_slice_in_dim(weight_in, begin, hidden_block, 1)
        return jnp.dot(left, right.T, preferred_element_type=jnp.float32)

    grad_tokens = rounded_sum(input_term, N_COL, (TOKENS, D)).astype(jnp.bfloat16)
    return (output, grad_tokens, grad_in, grad_out)
```

```python
import jax
import jax.numpy as jnp
from jax import lax
from jax.sharding import PartitionSpec as P

tanh_gain = 0.7978845608028654
cubic_term = 0.044715
side = 4
planes = 8


def gelu_parts(hidden):
    squared = hidden * hidden
    tangent = jnp.tanh(tanh_gain * (hidden + cubic_term * squared * hidden))
    value = 0.5 * hidden * (1.0 + tangent)
    slope = 0.5 * (1.0 + tangent) + 0.5 * hidden * (1.0 - tangent * tangent) * tanh_gain * (
        1.0 + 3.0 * cubic_term * squared
    )
    return value, slope


def contract_rows(left, right):
    return lax.dot_general(
        left, right, (((0,), (0,)), ((), ())), preferred_element_type=jnp.float32
    )


def contract_cols(left, right):
    return lax.dot_general(
        left, right, (((1,), (1,)), ((), ())), preferred_element_type=jnp.float32
    )


def device(x, y, z, core):
    return ((x % side) * side + y % side) * (planes * 2) + z * 2 + core


def ring_pairs(first, shift):
    pairs = []
    for x in range(side):
        for y in range(side):
            for z in range(planes):
                for core in range(2):
                    along_x = (core == 0) == first
                    to = device(x + shift, y, z, core) if along_x else device(x, y + shift, z, core)
                    pairs.append((device(x, y, z, core), to))
    return pairs


ring_shift = {
    (first, shift): ring_pairs(first, shift) for first in (True, False) for shift in (1, 2, 3)
}
core_pairs = [(i, i ^ 1) for i in range(planes * 2)]
plane_groups = [[z * 2 + core for z in range(planes)] for core in range(2)]
both = ("row", "col")


def other_core(block):
    return lax.ppermute(block, "col", core_pairs)


def over_planes(blocks):
    return lax.all_to_all(blocks, "col", 0, 0, tiled=True, axis_index_groups=plane_groups)


def gather_tokens(block):
    rows, width = block.shape
    mine = over_planes(jnp.broadcast_to(block[None], (planes, rows, width)))
    mine = mine.reshape(planes * rows, width)
    return jnp.concatenate([mine, other_core(mine)], axis=0)


def scatter_tokens(partial):
    half, width = partial.shape[0] // 2, partial.shape[1]
    pair = partial[:half].astype(jnp.float32) + other_core(partial[half:]).astype(jnp.float32)
    blocks = pair.astype(jnp.bfloat16).reshape(planes, half // planes, width)
    return jnp.sum(over_planes(blocks).astype(jnp.float32), axis=0).astype(jnp.bfloat16)


def ring_reduce(partial, place, first):
    blocks = partial.reshape(side, partial.shape[0] // side, partial.shape[1])
    came = [
        lax.ppermute(
            lax.dynamic_index_in_dim(blocks, (place + shift) % side, 0, keepdims=False),
            both,
            ring_shift[first, shift],
        )
        for shift in (1, 3, 2)
    ]
    total = lax.dynamic_index_in_dim(blocks, place, 0, keepdims=False).astype(jnp.float32)
    for block in came:
        total = total + block.astype(jnp.float32)
    return total


def ring_gather(block, place, first):
    rows, width = block.shape
    whole = jnp.zeros((side, rows, width), block.dtype)
    whole = lax.dynamic_update_index_in_dim(whole, block, place, 0)
    for shift in (1, 3, 2):
        came = lax.ppermute(block, both, ring_shift[first, shift])
        whole = lax.dynamic_update_index_in_dim(whole, came, (place - shift) % side, 0)
    return whole.reshape(side * rows, width)


def local(tokens, weight_in, weight_out, cotangent):
    chip, core = lax.axis_index("row"), lax.axis_index("col") % 2
    x, y = chip // side, chip % side
    place_one, place_two = jnp.where(core == 0, x, y), jnp.where(core == 0, y, x)

    def reduce_features(partial):
        total = ring_reduce(partial, place_one, True)
        return ring_reduce(total.astype(jnp.bfloat16), place_two, False)

    def gather_features(block):
        return ring_gather(ring_gather(block, place_two, False), place_one, True)

    token_block = gather_tokens(tokens)
    grad_block = gather_tokens(cotangent)
    grad_scale = token_block.shape[0] ** (-0.5)
    partial_value = jnp.dot(token_block, weight_in, preferred_element_type=jnp.float32)
    hidden = reduce_features(partial_value.astype(jnp.bfloat16))
    value, slope = gelu_parts(hidden)
    activation = gather_features(value.astype(jnp.bfloat16))
    grad_partial = contract_cols(grad_block, weight_out)
    grad_activation = reduce_features(grad_partial.astype(jnp.bfloat16))
    grad_hidden = gather_features((grad_activation * slope).astype(jnp.bfloat16))
    output = scatter_tokens(
        jnp.dot(activation, weight_out, preferred_element_type=jnp.float32).astype(jnp.bfloat16)
    )
    grad_out = (contract_rows(activation, grad_block) * grad_scale).astype(jnp.bfloat16)
    grad_tokens = scatter_tokens(contract_cols(grad_hidden, weight_in).astype(jnp.bfloat16))
    grad_in = (contract_rows(token_block, grad_hidden) * grad_scale).astype(jnp.bfloat16)
    return (output, grad_tokens, grad_in, grad_out)


def solution(mesh):
    in_specs = (P("col", "row"), P("row", "col"), P("col", "row"), P("col", "row"))
    out_specs = (P("col", "row"), P("col", "row"), P("row", "col"), P("col", "row"))
    return jax.shard_map(local, mesh=mesh, in_specs=in_specs, out_specs=out_specs, check_vma=False)
```

```python
import jax
import jax.numpy as jnp
from jax import lax
from jax.sharding import PartitionSpec as P

tanh_gain = 0.7978845608028654
cubic_term = 0.044715
side = 4
planes = 8
chunks = ((4, 3, -3, -2), (2, 1, -1, 0))
both = ("row", "col")


def gelu_parts(hidden):
    squared = hidden * hidden
    tangent = jnp.tanh(tanh_gain * (hidden + cubic_term * squared * hidden))
    value = 0.5 * hidden * (1.0 + tangent)
    slope = 0.5 * (1.0 + tangent) + 0.5 * hidden * (1.0 - tangent * tangent) * tanh_gain * (
        1.0 + 3.0 * cubic_term * squared
    )
    return value, slope


def contract_rows(left, right):
    return lax.dot_general(
        left, right, (((0,), (0,)), ((), ())), preferred_element_type=jnp.float32
    )


def contract_cols(left, right):
    return lax.dot_general(
        left, right, (((1,), (1,)), ((), ())), preferred_element_type=jnp.float32
    )


def device(x, y, z, core):
    return (x * side + y) * (planes * 2) + z * 2 + core


def ring_pairs(first, flip):
    pairs = []
    for x in range(side):
        for y in range(side):
            for z in range(planes):
                for core in range(2):
                    along_x = (core == 0) == first
                    to = device(x ^ flip, y, z, core) if along_x else device(x, y ^ flip, z, core)
                    pairs.append((device(x, y, z, core), to))
    return pairs


flips = (1, 3, 2)
ring = {(first, flip): ring_pairs(first, flip) for first in (True, False) for flip in flips}
core_pairs = [(i, i ^ 1) for i in range(planes * 2)]


def other_core(block):
    return lax.ppermute(block, "col", core_pairs)


def to_plane(block, ahead):
    if ahead == 0:
        return block
    pairs = [(i, (i + 2 * ahead) % (planes * 2)) for i in range(planes * 2)]
    return lax.ppermute(block, "col", pairs)


def after(value, *others):
    return lax.optimization_barrier((value, others))[0]


def ring_send(blocks, place, first):
    return [
        lax.ppermute(
            lax.dynamic_index_in_dim(blocks, place ^ flip, 1, keepdims=False), both, ring[first, flip]
        )
        for flip in flips
    ]


def ring_sum(blocks, place, came):
    total = lax.dynamic_index_in_dim(blocks, place, 1, keepdims=False).astype(jnp.float32)
    for block in came:
        total = total + block.astype(jnp.float32)
    return total


def ring_share(block, first):
    return [lax.ppermute(block, both, ring[first, flip]) for flip in flips]


def ring_join(block, place, came):
    count, rows, width = block.shape
    whole = jnp.zeros((count, side, rows, width), block.dtype)
    whole = lax.dynamic_update_index_in_dim(whole, block, place, 1)
    for flip, piece in zip(flips, came):
        whole = lax.dynamic_update_index_in_dim(whole, piece, place ^ flip, 1)
    return whole.reshape(count, side * rows, width)


def local(tokens, weight_in, weight_out, cotangent):
    chip, core = lax.axis_index("row"), lax.axis_index("col") % 2
    x, y = chip // side, chip % side
    place_one, place_two = jnp.where(core == 0, x, y), jnp.where(core == 0, y, x)
    rows, width = tokens.shape
    hidden_width = weight_in.shape[1]
    grad_scale = (rows * planes * 2) ** (-0.5)
    half = planes // 2 * rows

    pair = jnp.stack([tokens, cotangent])
    order = chunks[0] + chunks[1]
    mine = lax.optimization_barrier([to_plane(pair, -ahead) for ahead in order])
    mine = jnp.stack(mine, axis=1).reshape(2, 2, half, width)
    gathered = jnp.stack([mine, other_core(mine)], axis=2).reshape(2, 4 * half, width)

    def project(chunk):
        rows_here = slice(chunk * 2 * half, (chunk + 1) * 2 * half)
        value_part = jnp.dot(gathered[0, rows_here], weight_in, preferred_element_type=jnp.float32)
        grad_part = contract_cols(gathered[1, rows_here], weight_out)
        parts = jnp.stack([value_part.astype(jnp.bfloat16), grad_part.astype(jnp.bfloat16)])
        return parts.reshape(2, side, -1, hidden_width)

    def middle(parts, came):
        parts = ring_sum(parts, place_one, came).astype(jnp.bfloat16)
        return parts.reshape(2, side, -1, hidden_width)

    def activate(parts, came):
        hidden, grad_activation = ring_sum(parts, place_two, came)
        value, slope = gelu_parts(hidden)
        return jnp.stack([value.astype(jnp.bfloat16), (grad_activation * slope).astype(jnp.bfloat16)])

    def project_back(acts):
        output_part = jnp.dot(acts[0], weight_out, preferred_element_type=jnp.float32)
        input_part = contract_cols(acts[1], weight_in)
        return jnp.stack([output_part.astype(jnp.bfloat16), input_part.astype(jnp.bfloat16)])

    def fold(parts):
        parts = parts[:, :half].astype(jnp.float32) + other_core(parts[:, half:]).astype(jnp.float32)
        return parts.astype(jnp.bfloat16).reshape(2, planes // 2, rows, width)

    def send_back(parts, chunk):
        return [to_plane(parts[:, i], ahead) for i, ahead in enumerate(chunks[chunk])]

    a_part = project(0)
    a_came = ring_send(a_part, place_one, True)
    b_part = project(1)
    b_came = ring_send(b_part, place_one, True)
    a_mid = middle(a_part, a_came)
    a_came = ring_send(a_mid, place_two, False)
    b_mid = middle(b_part, after(b_came, a_came))
    b_came = ring_send(b_mid, place_two, False)
    a_act = activate(a_mid, a_came)
    a_came = ring_share(a_act, False)
    b_act = activate(b_mid, after(b_came, a_came))
    b_came = ring_share(b_act, False)
    a_act = ring_join(a_act, place_two, a_came)
    a_came = ring_share(a_act, True)
    b_act = ring_join(b_act, place_two, b_came)
    b_came = ring_share(b_act, True)
    a_act = ring_join(a_act, place_one, a_came)
    a_back = fold(project_back(a_act))
    b_act = ring_join(b_act, place_one, after(b_came, a_back))
    a_sent = send_back(a_back, 0)
    b_back = fold(project_back(b_act))
    b_sent = send_back(b_back, 1)

    total = a_sent[0].astype(jnp.float32)
    for block in a_sent[1:] + b_sent:
        total = total + block.astype(jnp.float32)
    total = total.astype(jnp.bfloat16)
    acts = jnp.concatenate([a_act, b_act], axis=1)
    grad_out = (contract_rows(acts[0], gathered[1]) * grad_scale).astype(jnp.bfloat16)
    grad_in = (contract_rows(gathered[0], acts[1]) * grad_scale).astype(jnp.bfloat16)
    return (total[0], total[1], grad_in, grad_out)


def solution(mesh):
    in_specs = (P("col", "row"), P("row", "col"), P("col", "row"), P("col", "row"))
    out_specs = (P("col", "row"), P("col", "row"), P("row", "col"), P("col", "row"))
    return jax.shard_map(local, mesh=mesh, in_specs=in_specs, out_specs=out_specs, check_vma=False)
```

```python
import jax
import jax.numpy as jnp
from jax import lax
from jax.sharding import PartitionSpec as P

tanh_gain = 0.7978845608028654
cubic_term = 0.044715
side = 4
planes = 8
order = (0, 1, 2, 6, 7, 3, 5, 4)
sent_order = (1, 2, 4, 5, 3, 7, 6)
both = ("row", "col")


def gelu_parts(hidden):
    squared = hidden * hidden
    tangent = jnp.tanh(tanh_gain * (hidden + cubic_term * squared * hidden))
    value = 0.5 * hidden * (1.0 + tangent)
    slope = 0.5 * (1.0 + tangent) + 0.5 * hidden * (1.0 - tangent * tangent) * tanh_gain * (
        1.0 + 3.0 * cubic_term * squared
    )
    return value, slope


def contract_rows(left, right):
    return lax.dot_general(
        left, right, (((0,), (0,)), ((), ())), preferred_element_type=jnp.float32
    )


def contract_cols(left, right):
    return lax.dot_general(
        left, right, (((1,), (1,)), ((), ())), preferred_element_type=jnp.float32
    )


def device(x, y, z, core):
    return (x * side + y) * (planes * 2) + z * 2 + core


def ring_pairs(first, flip):
    pairs = []
    for x in range(side):
        for y in range(side):
            for z in range(planes):
                for core in range(2):
                    along_x = (core == 0) == first
                    to = device(x ^ flip, y, z, core) if along_x else device(x, y ^ flip, z, core)
                    pairs.append((device(x, y, z, core), to))
    return pairs


flips = (1, 3, 2)
ring = {(first, flip): ring_pairs(first, flip) for first in (True, False) for flip in flips}
core_pairs = [(i, i ^ 1) for i in range(planes * 2)]


def other_core(block):
    return lax.ppermute(block, "col", core_pairs)


def to_plane(block, flip):
    if flip == 0:
        return block
    return lax.ppermute(block, "col", [(i, i ^ (2 * flip)) for i in range(planes * 2)])


def after(value, *others):
    return lax.optimization_barrier((value, others))[0]


def ring_send(blocks, place, first):
    pieces = [
        lax.dynamic_index_in_dim(blocks, place ^ flip, 1, keepdims=False) for flip in flips + (0,)
    ]
    pieces = lax.optimization_barrier(pieces)
    came = [lax.ppermute(piece, both, ring[first, flip]) for flip, piece in zip(flips, pieces)]
    return came + pieces[3:]


def ring_sum(came):
    total = came[-1].astype(jnp.float32)
    for block in came[:-1]:
        total = total + block.astype(jnp.float32)
    return total


def ring_share(block, first):
    return [lax.ppermute(block, both, ring[first, flip]) for flip in flips]


def ring_join(block, place, came):
    axis = block.ndim - 2
    whole = jnp.zeros(block.shape[:axis] + (side,) + block.shape[axis:], block.dtype)
    whole = lax.dynamic_update_index_in_dim(whole, block, place, axis)
    for flip, piece in zip(flips, came):
        whole = lax.dynamic_update_index_in_dim(whole, piece, place ^ flip, axis)
    return whole.reshape(block.shape[:axis] + (-1, block.shape[-1]))


def local(tokens, weight_in, weight_out, cotangent):
    chip, core = lax.axis_index("row"), lax.axis_index("col") % 2
    x, y = chip // side, chip % side
    place_one, place_two = jnp.where(core == 0, x, y), jnp.where(core == 0, y, x)
    rows, width = tokens.shape
    hidden_width = weight_in.shape[1]
    grad_scale = (rows * planes * 2) ** (-0.5)

    def project(block):
        value_part = jnp.dot(block[0], weight_in, preferred_element_type=jnp.float32)
        grad_part = contract_cols(block[1], weight_out)
        parts = jnp.stack([value_part.astype(jnp.bfloat16), grad_part.astype(jnp.bfloat16)])
        return parts.reshape(2, side, -1, hidden_width)

    def project_back(acts):
        output_part = jnp.dot(acts[0], weight_out, preferred_element_type=jnp.float32)
        return output_part, contract_cols(acts[1], weight_in)

    pair = jnp.stack([tokens, cotangent])
    mine = lax.optimization_barrier([to_plane(pair, flip) for flip in order])
    own = jnp.stack(mine, axis=1).reshape(2, planes * rows, width)
    other = other_core(own)

    own_part = project(own)
    own_came = ring_send(own_part, place_one, True)
    other_part = project(after(other, own_part))
    other_came = ring_send(other_part, place_one, True)
    own_sum = ring_sum(own_came).astype(jnp.bfloat16)
    other_sum = ring_sum(other_came).astype(jnp.bfloat16)
    sums = [part.reshape(2, side, -1, hidden_width) for part in (own_sum, other_sum)]

    def pick(place):
        return jnp.stack(
            [lax.dynamic_index_in_dim(part, place, 1, keepdims=False) for part in sums]
        )

    came = [lax.ppermute(pick(place_two ^ flip), both, ring[False, flip]) for flip in flips]
    sums = pick(place_two).astype(jnp.float32)
    for block in came:
        sums = sums + block.astype(jnp.float32)
    value, slope = gelu_parts(sums[:, 0])
    acts = jnp.stack([value, sums[:, 1] * slope], axis=1).astype(jnp.bfloat16)
    acts = ring_join(acts, place_two, ring_share(acts, False))
    acts = ring_join(acts, place_one, ring_share(acts, True))
    other_back = jnp.stack(project_back(acts[1])).astype(jnp.bfloat16)
    own_act = after(acts[0], other_back)
    back = jnp.stack(project_back(own_act)) + other_core(other_back).astype(jnp.float32)
    back = back.astype(jnp.bfloat16).reshape(2, planes, rows, width)
    came = {flip: to_plane(back[:, order.index(flip)], flip) for flip in sent_order}

    acts = after(jnp.concatenate([acts[0], acts[1]], axis=1), came[1], came[2])
    gathered = jnp.concatenate([own, other], axis=1)
    grad_out = (contract_rows(acts[0], gathered[1]) * grad_scale).astype(jnp.bfloat16)
    grad_in = (contract_rows(gathered[0], acts[1]) * grad_scale).astype(jnp.bfloat16)
    total = after(back[:, order.index(0)], grad_in, grad_out).astype(jnp.float32)
    for flip in sent_order:
        total = total + came[flip].astype(jnp.float32)
    total = total.astype(jnp.bfloat16)
    return (total[0], total[1], grad_in, grad_out)


def solution(mesh):
    in_specs = (P("col", "row"), P("row", "col"), P("col", "row"), P("col", "row"))
    out_specs = (P("col", "row"), P("col", "row"), P("row", "col"), P("col", "row"))
    return jax.shard_map(local, mesh=mesh, in_specs=in_specs, out_specs=out_specs, check_vma=False)
```

```python
import jax
import jax.numpy as jnp
from jax import lax
from jax.sharding import PartitionSpec as P

tanh_gain = 0.7978845608028654
cubic_term = 0.044715
side = 4
planes = 8
order = (0, 1, -1, 2, -2, 3, -3, 4)
sent_order = (1, -1, 4, -3, 3, -2, 2)
both = ("row", "col")


def gelu_parts(hidden):
    squared = hidden * hidden
    tangent = jnp.tanh(tanh_gain * (hidden + cubic_term * squared * hidden))
    value = 0.5 * hidden * (1.0 + tangent)
    slope = 0.5 * (1.0 + tangent) + 0.5 * hidden * (1.0 - tangent * tangent) * tanh_gain * (
        1.0 + 3.0 * cubic_term * squared
    )
    return value, slope


def contract_rows(left, right):
    return lax.dot_general(
        left, right, (((0,), (0,)), ((), ())), preferred_element_type=jnp.float32
    )


def contract_cols(left, right):
    return lax.dot_general(
        left, right, (((1,), (1,)), ((), ())), preferred_element_type=jnp.float32
    )


def device(x, y, z, core):
    return (x * side + y) * (planes * 2) + z * 2 + core


def ring_pairs(first, flip):
    pairs = []
    for x in range(side):
        for y in range(side):
            for z in range(planes):
                for core in range(2):
                    along_x = (core == 0) == first
                    to = device(x ^ flip, y, z, core) if along_x else device(x, y ^ flip, z, core)
                    pairs.append((device(x, y, z, core), to))
    return pairs


flips = (1, 3, 2)
ring = {(first, flip): ring_pairs(first, flip) for first in (True, False) for flip in flips}
core_pairs = [(i, i ^ 1) for i in range(planes * 2)]


def other_core(block):
    return lax.ppermute(block, "col", core_pairs)


def to_plane(block, ahead):
    if ahead == 0:
        return block
    return lax.ppermute(block, "col", [(i, (i + 2 * ahead) % (planes * 2)) for i in range(planes * 2)])


def after(value, *others):
    return lax.optimization_barrier((value, others))[0]


def ring_send(blocks, place, first):
    pieces = [
        lax.dynamic_index_in_dim(blocks, place ^ flip, 1, keepdims=False) for flip in flips + (0,)
    ]
    pieces = lax.optimization_barrier(pieces)
    came = [lax.ppermute(piece, both, ring[first, flip]) for flip, piece in zip(flips, pieces)]
    return came + pieces[3:]


def ring_sum(came):
    total = came[-1].astype(jnp.float32)
    for block in came[:-1]:
        total = total + block.astype(jnp.float32)
    return total


def ring_share(block, first):
    return [lax.ppermute(block, both, ring[first, flip]) for flip in flips]


def ring_join(block, place, came):
    axis = block.ndim - 2
    whole = jnp.zeros(block.shape[:axis] + (side,) + block.shape[axis:], block.dtype)
    whole = lax.dynamic_update_index_in_dim(whole, block, place, axis)
    for flip, piece in zip(flips, came):
        whole = lax.dynamic_update_index_in_dim(whole, piece, place ^ flip, axis)
    return whole.reshape(block.shape[:axis] + (-1, block.shape[-1]))


def local(tokens, weight_in, weight_out, cotangent):
    chip, core = lax.axis_index("row"), lax.axis_index("col") % 2
    x, y = chip // side, chip % side
    place_one, place_two = jnp.where(core == 0, x, y), jnp.where(core == 0, y, x)
    rows, width = tokens.shape
    hidden_width = weight_in.shape[1]
    grad_scale = (rows * planes * 2) ** (-0.5)

    def project(block):
        value_part = jnp.dot(block[0], weight_in, preferred_element_type=jnp.float32)
        grad_part = contract_cols(block[1], weight_out)
        parts = jnp.stack([value_part.astype(jnp.bfloat16), grad_part.astype(jnp.bfloat16)])
        return parts.reshape(2, side, -1, hidden_width)

    def project_back(acts):
        output_part = jnp.dot(acts[0], weight_out, preferred_element_type=jnp.float32)
        return output_part, contract_cols(acts[1], weight_in)

    pair = jnp.stack([tokens, cotangent])
    mine = lax.optimization_barrier([to_plane(pair, -ahead) for ahead in order])
    own = jnp.stack(mine, axis=1).reshape(2, planes * rows, width)
    other = other_core(own)

    own_part = project(own)
    own_came = ring_send(own_part, place_one, True)
    other_part = project(after(other, own_part))
    other_came = ring_send(other_part, place_one, True)
    own_sum = ring_sum(own_came).astype(jnp.bfloat16)
    other_sum = ring_sum(other_came).astype(jnp.bfloat16)
    sums = [part.reshape(2, side, -1, hidden_width) for part in (own_sum, other_sum)]

    def pick(place):
        return jnp.stack(
            [lax.dynamic_index_in_dim(part, place, 1, keepdims=False) for part in sums]
        )

    came = [lax.ppermute(pick(place_two ^ flip), both, ring[False, flip]) for flip in flips]
    sums = pick(place_two).astype(jnp.float32)
    for block in came:
        sums = sums + block.astype(jnp.float32)
    value, slope = gelu_parts(sums[:, 0])
    acts = jnp.stack([value, sums[:, 1] * slope], axis=1).astype(jnp.bfloat16)
    acts = ring_join(acts, place_two, ring_share(acts, False))
    acts = ring_join(acts, place_one, ring_share(acts, True))
    other_back = jnp.stack(project_back(acts[1])).astype(jnp.bfloat16)
    own_act = after(acts[0], other_back)
    back = jnp.stack(project_back(own_act)) + other_core(other_back).astype(jnp.float32)
    back = back.astype(jnp.bfloat16).reshape(2, planes, rows, width)
    came = {ahead: to_plane(back[:, order.index(ahead)], ahead) for ahead in sent_order}

    acts = after(jnp.concatenate([acts[0], acts[1]], axis=1), came[1], came[-1])
    gathered = jnp.concatenate([own, other], axis=1)
    grad_out = (contract_rows(acts[0], gathered[1]) * grad_scale).astype(jnp.bfloat16)
    grad_in = (contract_rows(gathered[0], acts[1]) * grad_scale).astype(jnp.bfloat16)
    total = after(back[:, order.index(0)], grad_in, grad_out).astype(jnp.float32)
    for ahead in sent_order:
        total = total + came[ahead].astype(jnp.float32)
    total = total.astype(jnp.bfloat16)
    return (total[0], total[1], grad_in, grad_out)


def solution(mesh):
    in_specs = (P("col", "row"), P("row", "col"), P("col", "row"), P("col", "row"))
    out_specs = (P("col", "row"), P("col", "row"), P("row", "col"), P("col", "row"))
    return jax.shard_map(local, mesh=mesh, in_specs=in_specs, out_specs=out_specs, check_vma=False)
```
